32 devices in a mesh: wide: 4 (over x, core), col: 8 (over z, y).
Axes of the slice: x: 2, y: 2, z: 4, core: 2. Of those that a mesh axis runs over, the one named last changes fastest.
Arguments:
- adjoint: bfloat16 [32, 1536], P(None, ('wide', 'col')), may hold values from -6 to 6
- operator: bfloat16 [1536, 196608], P('wide', 'col'), may hold values from -0.21875 to 0.21875
- owner: int32 [196608], P(('col', 'wide')), may hold values from 0 to 196607, as said below
Outputs:
- junction_sums: float32 [32, 196608], P(None, ('col', 'wide'))
The draws below stay inside these ranges and needn't reach their ends.
Inputs may be any that keep to these rules, and one draw needn't show every extreme that they name: Unknown j of device block b = j // 6144 (blocks ordered col first, then wide) has owner j itself, or is a duplicate whose owner is an unknown in the lower half of a block of the same index of col; duplicates lie only in the upper half of a block and owners of duplicates are never duplicates. One block hands at most 16 duplicates to the blocks of any one index of wide, and this count is reached in every draw, by some block towards every index of wide and towards some index of wide from every block.
All inputs are finite; a program needn't handle non-finite values.
Results may differ from the reference program's by a relative error of at most 0.0003.
Values may be sent and summed in bfloat16 or wider, within the bound.
A program may use at most 64 MiB of HBM per device.

```python
import jax
import jax.numpy as jnp
from jax import lax

N = 196608
NRHS = 32
RD = 384
CAP = 16
ROWS = 1536
PIECE = 6144
N_WIDE = 4
N_COL = 8


def draw_owner(key, part):
    wide_count = N_WIDE
    col_count = N_COL
    half_piece = PIECE // 2
    key_heavy, key_recv, key_counts, key_target, key_perm = jax.random.split(key, 5)
    heavy_send = jax.random.randint(key_heavy, (col_count,), 0, wide_count)
    heavy_recv = jax.random.randint(key_recv, (col_count,), 0, wide_count)
    counts = jax.random.randint(key_counts, (col_count, wide_count, wide_count), CAP // 4, CAP + 1)
    peers = jnp.arange(wide_count, dtype=jnp.int32)
    send_mask = peers[None, :] == heavy_send[:, None]
    recv_mask = peers[None, :] == heavy_recv[:, None]
    counts = jnp.where(send_mask[:, :, None], CAP, counts)
    counts = jnp.where(recv_mask[:, None, :], CAP, counts)
    ends = jnp.cumsum(counts, axis=2)
    starts = ends - counts
    slots = jnp.arange(half_piece, dtype=jnp.int32)
    inside = (slots[None, None, None, :] >= starts[..., None]) & (slots[None, None, None, :] < ends[..., None])
    inside_int = inside.astype(jnp.int32)
    repeated = jnp.sum(inside_int, axis=2) > 0
    target_peer = jnp.sum(inside_int * peers[None, None, :, None], axis=2)
    targets = jax.random.randint(key_target, (col_count, wide_count, half_piece), 0, half_piece)
    col_base = (jnp.arange(col_count, dtype=jnp.int32) * (wide_count * PIECE))[:, None, None]
    wide_base = (peers * PIECE)[None, :, None]
    perm_keys = jax.random.split(key_perm, col_count * wide_count)
    perms = jax.vmap(lambda k: jax.random.permutation(k, half_piece))(perm_keys).astype(jnp.int32)
    perms = perms.reshape(col_count, wide_count, half_piece)
    self_cols = col_base + wide_base + half_piece + perms
    values = jnp.where(repeated, col_base + target_peer * PIECE + targets, self_cols)

    def place(order, vals):
        return jnp.zeros((half_piece,), jnp.int32).at[order].set(vals)
    upper = jax.vmap(place)(perms.reshape(-1, half_piece), values.reshape(-1, half_piece))
    upper = upper.reshape(col_count, wide_count, half_piece)
    lower = col_base + wide_base + slots[None, None, :]
    lower = jnp.broadcast_to(lower, (col_count, wide_count, half_piece))
    return jnp.concatenate([lower, upper], axis=2).reshape(-1).astype(jnp.int32)


def with_spikes(values, rng, source, target, blocks, factor):
    owner, partner = [(jnp.arange(values.shape[axis_at]) // (values.shape[axis_at] // blocks)).reshape([-1 if axis == axis_at else 1 for axis in range(values.ndim)]) for axis_at in (source, target)]
    chosen = jax.random.permutation(rng, blocks)[partner]
    strong = (owner == chosen) | (owner == (partner + blocks // 2) % blocks)
    return jnp.where(strong, factor * values, values)


def level_of(key, extent, pieces, least, largest):
    def one(position, blocks):
        draws = jax.random.uniform(jax.random.fold_in(jax.random.fold_in(key, 6), position), (blocks,), jnp.float32, least / len(pieces), largest / len(pieces))
        return jnp.repeat(jnp.exp(draws), extent[position] // blocks).reshape((-1,) + (1,) * (len(extent) - position - 1))

    level = one(*pieces[0])
    for cut in pieces[1:]:
        level = level * one(*cut)
    return level


def bell_draw(rng, dims, scale, most, shards=(), kind=jnp.bfloat16):
    level = level_of(rng, dims, shards, -0.22, 0.18) if shards else 1.0
    entries = jax.random.normal(rng, dims, jnp.float32) * scale * level
    return jnp.minimum(jnp.maximum(entries, -most), most).astype(kind)


def gaussian_with(key, shape, deviation, reach, cuts, heavy, kind=jnp.bfloat16):
    result = deviation * jax.random.normal(key, shape, jnp.float32)
    if cuts:
        result = result * level_of(key, shape, cuts, -0.22, 0.18)
    return jnp.clip(with_spikes(result, jax.random.fold_in(key, 3), *heavy), -reach, reach).astype(kind)


def setup_inputs(seed: int = 0) -> dict:
    key_of = jax.random.split(jax.random.key(seed), 4)
    return {
        "adjoint": bell_draw(key_of[0], (NRHS, ROWS), 1.0, 6.0, ((1, 32),)),
        "operator": gaussian_with(key_of[1], (ROWS, N), ROWS ** -0.5, 0.21875, ((0, 4), (1, 8)), (0, 1, 8, 2.0)),
        "owner": draw_owner(jax.random.fold_in(key_of[3], 71), 0),
    }


def reference(adjoint, operator, owner):
    block_rows = RD
    count = ROWS // block_rows

    def accumulate(carry, index):
        start = (index * block_rows).astype(jnp.int32)
        rows_x = lax.dynamic_slice_in_dim(adjoint, start, block_rows, 1)
        rows_a = lax.dynamic_slice_in_dim(operator, start, block_rows, 0)
        return carry + jnp.dot(rows_x, rows_a, preferred_element_type=jnp.float32), None

    partials, unused = lax.scan(accumulate, jnp.zeros((NRHS, N), jnp.float32), jnp.arange(count, dtype=jnp.int32))
    summed = jax.ops.segment_sum(partials.T, owner, num_segments=N)
    return summed.T
```

```python
import functools

import jax
import jax.numpy as jnp
from jax import lax
from jax.experimental import pallas as pl
from jax.experimental.pallas import tpu as pltpu
from jax.sharding import PartitionSpec as P

CAP = 16
LANES = 128
MESH = pl.DeviceIdType.MESH
F32 = jnp.float32
BF16 = jnp.bfloat16


def split(x):
    high = x.astype(BF16)
    low = (x - high.astype(F32)).astype(BF16)
    return jnp.concatenate([high, low], axis=0)


def kernel(
    wide_count, col_count, chunks,
    adj_ref, op_ref, own_ref, out_ref,
    op_buf, adj_buf, a_buf, owners, sib_out, sib_in, mine, far_in, hot, place_buf, dup_out, dup_in,
    op_sem, adj_send, adj_recv, own_send, own_recv, sib_send, sib_recv, far_send, far_recv, dup_send, dup_recv,
):
    chips = wide_count // 2
    sensors, depth = adj_ref.shape
    rows, width, chunk = op_buf.shape[1], out_ref.shape[1], op_buf.shape[2]
    half = width // 2
    half_rows = half // LANES
    slots = wide_count * CAP
    all_slots = chips * slots
    w, k = lax.axis_index("wide"), lax.axis_index("col")
    g, c = w // 2, lax.rem(w, 2)

    def ahead(e, other):
        return lax.rem(g + e, chips) * 2 + (1 - c if other else c)

    steps = [(e, q) for e in list(range(1, chips)) + [0] for q in range(chunks)]
    loads = []
    for n, (e, q) in enumerate(steps):
        for other in (1, 0):
            start = pl.multiple_of(ahead(e, other) * width + q * chunk, LANES)
            i = 2 * n + 1 - other
            load = pltpu.make_async_copy(op_ref.at[:, pl.ds(start, chunk)], op_buf.at[i], op_sem.at[i])
            load.start()
            loads.append(load)

    adj_buf[k] = jnp.zeros(adj_buf.shape[1:], BF16)
    adj_buf[k, :, :depth] = adj_ref[...]
    pairs = [(e, other) for e in range(chips) for other in (0, 1)][1:]

    barrier = pltpu.get_barrier_semaphore()
    for d in range(1, col_count):
        pl.semaphore_signal(barrier, inc=1, device_id={"col": lax.rem(k + d, col_count)}, device_id_type=MESH)
    for e, other in pairs:
        pl.semaphore_signal(barrier, inc=1, device_id={"wide": ahead(e, other)}, device_id_type=MESH)
    pl.semaphore_wait(barrier, col_count - 1 + wide_count - 1)

    adj_copies = []
    for d in range(1, col_count):
        copy = pltpu.make_async_remote_copy(
            adj_buf.at[k], adj_buf.at[k], adj_send.at[d - 1], adj_recv.at[d - 1],
            device_id={"col": lax.rem(k + d, col_count)}, device_id_type=MESH)
        copy.start()
        adj_copies.append(copy)
    own_copies = []
    for e, other in pairs:
        at = 2 * e + other
        copy = pltpu.make_async_remote_copy(
            own_ref, owners.at[at], own_send.at[at], own_recv.at[at],
            device_id={"wide": ahead(e, other)}, device_id_type=MESH)
        copy.start()
        own_copies.append(copy)

    for d in range(1, col_count):
        source = lax.rem(k - d + col_count, col_count)
        pltpu.make_async_remote_copy(
            adj_buf.at[source], adj_buf.at[source], adj_send.at[d - 1], adj_recv.at[d - 1],
            device_id={"col": source}, device_id_type=MESH).wait_recv()
    padded = adj_buf.shape[2]
    total = jnp.zeros((sensors, rows), F32)
    from_row = lax.broadcasted_iota(jnp.int32, (padded, rows), 0)
    to_row = lax.broadcasted_iota(jnp.int32, (padded, rows), 1)
    for i in range(col_count):
        shift = (from_row < depth) & (to_row == from_row + i * depth)
        total += jnp.dot(adj_buf[i], shift.astype(F32).astype(BF16), preferred_element_type=F32)
    a_buf[...] = total.astype(BF16)

    def product(i):
        loads[i].wait()
        return jnp.dot(a_buf[...], op_buf[i], preferred_element_type=F32)

    sent = []

    def combine(e, q):
        sib_copies[(e, q)].wait_recv()
        mine[e, q] += sib_in[e, q]
        if e > 0:
            copy = pltpu.make_async_remote_copy(
                mine.at[e, q], far_in.at[e - 1, q], far_send.at[e - 1, q], far_recv.at[e - 1, q],
                device_id={"wide": ahead(e, 0)}, device_id_type=MESH)
            copy.start()
            sent.append((e, q, copy))

    sib_copies = {}
    for n, (e, q) in enumerate(steps):
        sib_out[e, q] = product(2 * n)
        copy = pltpu.make_async_remote_copy(
            sib_out.at[e, q], sib_in.at[e, q], sib_send.at[e, q], sib_recv.at[e, q],
            device_id={"wide": ahead(0, 1)}, device_id_type=MESH)
        copy.start()
        sib_copies[(e, q)] = copy
        mine[e, q] = product(2 * n + 1)
        if n > 0:
            combine(*steps[n - 1])
    combine(*steps[-1])

    for copy in own_copies:
        copy.wait_recv()
    lane_in = lax.broadcasted_iota(jnp.int32, (LANES, LANES), 0)
    lane_out = lax.broadcasted_iota(jnp.int32, (LANES, LANES), 1)
    before = (lane_in < lane_out).astype(F32).astype(BF16)
    ones = jnp.ones((LANES, LANES), BF16)
    slot_ids = lax.broadcasted_iota(jnp.int32, (all_slots, LANES), 0).astype(F32)
    columns = (lax.broadcasted_iota(jnp.int32, (half_rows, LANES), 0) * LANES
               + lax.broadcasted_iota(jnp.int32, (half_rows, LANES), 1))

    def marks(owner, block):
        return owner != k * (width * wide_count) + block * width + half + columns

    for other in (0, 1):
        place = jnp.zeros((all_slots, LANES), F32)
        for e in range(chips):
            chip = lax.rem(g - e + chips, chips)
            block = chip * 2 + (1 - c if other else c)
            owner = own_ref[half_rows:, :] if (e, other) == (0, 0) else owners[2 * e + other, half_rows:, :]
            repeated = marks(owner, block)
            flags = repeated.astype(F32).astype(BF16)
            ranks = jnp.dot(flags, before, preferred_element_type=F32)
            counts = jnp.dot(flags, ones, preferred_element_type=F32)
            target = (owner - k * (width * wide_count) + 1).astype(F32)
            base = jnp.zeros((1, LANES), F32) + (chip * slots).astype(F32)
            for r in range(half_rows):
                slot = jnp.where(repeated[r : r + 1, :], ranks[r : r + 1, :] + base, -1.0)
                base = base + counts[r : r + 1, :]
                chosen = slot_ids == slot
                place = place + jnp.where(chosen, target[r : r + 1, :], 0.0)
                if other == 0:
                    hot[chip, :, r * LANES : (r + 1) * LANES] = chosen.astype(F32).astype(BF16)
        place_buf[other] = jnp.sum(place, axis=1, keepdims=True) - 1.0

    nt = (((1,), (1,)), ((), ()))
    picked = jnp.zeros((2 * sensors, all_slots), F32)
    for e in range(chips):
        for q in range(chunks // 2, chunks):
            start = (q - chunks // 2) * chunk
            picked += lax.dot_general(
                split(mine[e, q]), hot[lax.rem(g + e, chips), :, start : start + chunk], nt,
                preferred_element_type=F32)
    dup_out[...] = picked[:sensors] + picked[sensors:]
    dup_copies = []
    for e, other in pairs:
        at = 2 * e + other
        copy = pltpu.make_async_remote_copy(
            dup_out, dup_in.at[at], dup_send.at[at], dup_recv.at[at],
            device_id={"wide": ahead(e, other)}, device_id_type=MESH)
        copy.start()
        dup_copies.append(copy)
    repeated = marks(own_ref[half_rows:, :], w)
    kept = 1.0 - repeated.astype(F32)
    for copy in dup_copies:
        copy.wait_recv()
    sums = [dup_out[...], None]
    for e, other in pairs:
        value = dup_in[2 * e + other]
        sums[other] = value if sums[other] is None else sums[other] + value
    sums = [split(value) for value in sums]
    for q in range(chunks // 2):
        mine_at = (lax.broadcasted_iota(jnp.int32, (all_slots, chunk), 1) + (w * width + q * chunk)).astype(F32)
        for other in (0, 1):
            lands = (mine_at == place_buf[other]).astype(F32).astype(BF16)
            added = jnp.dot(sums[other], lands, preferred_element_type=F32)
            mine[0, q] += added[:sensors] + added[sensors:]

    for q in range(chunks):
        value = mine[0, q]
        for e, at, copy in sent:
            if at == q:
                copy.wait_recv()
                value = value + far_in[e - 1, q]
        if q >= chunks // 2:
            first = (q - chunks // 2) * chunk // LANES
            parts = []
            for r in range(chunk // LANES):
                keep = jnp.broadcast_to(kept[first + r : first + r + 1, :], (sensors, LANES))
                parts.append(jnp.where(keep > 0.5, value[:, r * LANES : (r + 1) * LANES], 0.0))
            value = jnp.concatenate(parts, axis=1)
        out_ref[:, q * chunk : (q + 1) * chunk] = value

    for copy in adj_copies + own_copies + dup_copies + list(sib_copies.values()) + [s[2] for s in sent]:
        copy.wait_send()


def local(adjoint, operator, owner):
    wide_count, col_count = lax.axis_size("wide"), lax.axis_size("col")
    chips = wide_count // 2
    sensors, depth = adjoint.shape
    rows, block_cols = operator.shape
    width = block_cols // wide_count
    half = width // 2
    chunks = 4 if half % (2 * LANES) == 0 else 2
    chunk = width // chunks
    padded = -(-depth // LANES) * LANES
    all_slots = chips * wide_count * CAP
    pieces = (chips, chunks, sensors, chunk)
    dma = pltpu.SemaphoreType.DMA
    vmem = pl.BlockSpec(memory_space=pltpu.VMEM)
    return pl.pallas_call(
        functools.partial(kernel, wide_count, col_count, chunks),
        out_shape=jax.ShapeDtypeStruct((sensors, width), F32),
        in_specs=[vmem, pl.BlockSpec(memory_space=pl.ANY), vmem],
        out_specs=vmem,
        scratch_shapes=[
            pltpu.VMEM((wide_count * chunks, rows, chunk), BF16),
            pltpu.VMEM((col_count, sensors, padded), BF16),
            pltpu.VMEM((sensors, rows), BF16),
            pltpu.VMEM((wide_count, width // LANES, LANES), jnp.int32),
            pltpu.VMEM(pieces, F32),
            pltpu.VMEM(pieces, F32),
            pltpu.VMEM(pieces, F32),
            pltpu.VMEM((chips - 1,) + pieces[1:], F32),
            pltpu.VMEM((chips, all_slots, half), BF16),
            pltpu.VMEM((2, all_slots, 1), F32),
            pltpu.VMEM((sensors, all_slots), F32),
            pltpu.VMEM((wide_count, sensors, all_slots), F32),
            dma((wide_count * chunks,)),
            dma((col_count - 1,)), dma((col_count - 1,)),
            dma((wide_count,)), dma((wide_count,)),
            dma(pieces[:2]), dma(pieces[:2]),
            dma((chips - 1, chunks)), dma((chips - 1, chunks)),
            dma((wide_count,)), dma((wide_count,)),
        ],
        compiler_params=pltpu.CompilerParams(
            collective_id=0, has_side_effects=True, vmem_limit_bytes=56 * 1024 * 1024),
        cost_estimate=pl.CostEstimate(
            flops=2 * sensors * rows * block_cols, bytes_accessed=2 * rows * block_cols, transcendentals=0),
    )(adjoint, operator, owner.reshape(width // LANES, LANES))


def solution(mesh):
    return jax.shard_map(
        local,
        mesh=mesh,
        in_specs=(P(None, ("wide", "col")), P("wide", "col"), P(("col", "wide"))),
        out_specs=P(None, ("col", "wide")),
        check_vma=False,
    )
```

```python
import functools

import jax
import jax.numpy as jnp
from jax import lax
from jax.experimental import pallas as pl
from jax.experimental.pallas import tpu as pltpu
from jax.sharding import PartitionSpec as P

CAP = 16
LANES = 128
LEVELS = 32767.0
MESH = pl.DeviceIdType.MESH
F32 = jnp.float32
BF16 = jnp.bfloat16


def split(x):
    high = x.astype(BF16)
    low = (x - high.astype(F32)).astype(BF16)
    return jnp.concatenate([high, low], axis=0)


def kernel(
    wide_count, col_count, chunks,
    adj_ref, op_ref, own_ref, out_ref,
    op_buf, adj_buf, a_buf, owners, sib_out, sib_in, mine, far_out, far_in, top_out, top_in, hot, lands, place_buf, dup_out, dup_in,
    op_sem, adj_send, adj_recv, own_send, own_recv, sib_send, sib_recv, far_send, far_recv, top_send, top_recv, dup_send, dup_recv,
):
    chips = wide_count // 2
    sensors, depth = adj_ref.shape
    rows, width, chunk = op_buf.shape[1], out_ref.shape[1], op_buf.shape[2]
    half = width // 2
    half_rows = half // LANES
    slots = wide_count * CAP
    all_slots = chips * slots
    w, k = lax.axis_index("wide"), lax.axis_index("col")
    g, c = w // 2, lax.rem(w, 2)

    def ahead(e, other):
        return lax.rem(g + e, chips) * 2 + (1 - c if other else c)

    steps = [(e, q) for e in list(range(1, chips)) + [0] for q in range(chunks)]
    loads = []
    for n, (e, q) in enumerate(steps):
        for other in (1, 0):
            start = pl.multiple_of(ahead(e, other) * width + q * chunk, LANES)
            i = 2 * n + 1 - other
            load = pltpu.make_async_copy(op_ref.at[:, pl.ds(start, chunk)], op_buf.at[i], op_sem.at[i])
            load.start()
            loads.append(load)

    adj_buf[k] = jnp.zeros(adj_buf.shape[1:], BF16)
    adj_buf[k, :, :depth] = adj_ref[...]
    pairs = [(e, other) for e in range(chips) for other in (0, 1)][1:]

    barrier = pltpu.get_barrier_semaphore()
    for d in range(1, col_count):
        pl.semaphore_signal(barrier, inc=1, device_id={"col": lax.rem(k + d, col_count)}, device_id_type=MESH)
    for e, other in pairs:
        pl.semaphore_signal(barrier, inc=1, device_id={"wide": ahead(e, other)}, device_id_type=MESH)
    pl.semaphore_wait(barrier, col_count - 1 + wide_count - 1)

    adj_copies = []
    for d in range(1, col_count):
        copy = pltpu.make_async_remote_copy(
            adj_buf.at[k], adj_buf.at[k], adj_send.at[d - 1], adj_recv.at[d - 1],
            device_id={"col": lax.rem(k + d, col_count)}, device_id_type=MESH)
        copy.start()
        adj_copies.append(copy)
    own_copies = []
    for e, other in pairs:
        at = 2 * e + other
        copy = pltpu.make_async_remote_copy(
            own_ref, owners.at[at], own_send.at[at], own_recv.at[at],
            device_id={"wide": ahead(e, other)}, device_id_type=MESH)
        copy.start()
        own_copies.append(copy)

    lane_in = lax.broadcasted_iota(jnp.int32, (LANES, LANES), 0)
    lane_out = lax.broadcasted_iota(jnp.int32, (LANES, LANES), 1)
    before = (lane_in < lane_out).astype(F32).astype(BF16)
    ones = jnp.ones((LANES, LANES), BF16)
    slot_ids = lax.broadcasted_iota(jnp.int32, (all_slots, LANES), 0).astype(F32)
    columns = (lax.broadcasted_iota(jnp.int32, (half_rows, LANES), 0) * LANES
               + lax.broadcasted_iota(jnp.int32, (half_rows, LANES), 1))

    def marks(owner, block):
        return owner != k * (width * wide_count) + block * width + half + columns

    def index(e, other):
        place = place_buf[other] if e > 0 else jnp.zeros((all_slots, LANES), F32)
        chip = lax.rem(g - e + chips, chips)
        block = chip * 2 + (1 - c if other else c)
        owner = own_ref[half_rows:, :] if (e, other) == (0, 0) else owners[2 * e + other, half_rows:, :]
        repeated = marks(owner, block)
        flags = repeated.astype(F32).astype(BF16)
        ranks = jnp.dot(flags, before, preferred_element_type=F32)
        counts = jnp.dot(flags, ones, preferred_element_type=F32)
        target = (owner - k * (width * wide_count) + 1).astype(F32)
        base = jnp.zeros((1, LANES), F32) + (chip * slots).astype(F32)
        for r in range(half_rows):
            slot = jnp.where(repeated[r : r + 1, :], ranks[r : r + 1, :] + base, -1.0)
            base = base + counts[r : r + 1, :]
            chosen = slot_ids == slot
            place = place + jnp.where(chosen, target[r : r + 1, :], 0.0)
            if other == 0:
                hot[chip, :, r * LANES : (r + 1) * LANES] = chosen.astype(F32).astype(BF16)
        place_buf[other] = place

    index(0, 0)

    for d in range(1, col_count):
        source = lax.rem(k - d + col_count, col_count)
        pltpu.make_async_remote_copy(
            adj_buf.at[source], adj_buf.at[source], adj_send.at[d - 1], adj_recv.at[d - 1],
            device_id={"col": source}, device_id_type=MESH).wait_recv()
    padded = adj_buf.shape[2]
    total = jnp.zeros((sensors, rows), F32)
    from_row = lax.broadcasted_iota(jnp.int32, (padded, rows), 0)
    to_row = lax.broadcasted_iota(jnp.int32, (padded, rows), 1)
    for i in range(col_count):
        shift = (from_row < depth) & (to_row == from_row + i * depth)
        total += jnp.dot(adj_buf[i], shift.astype(F32).astype(BF16), preferred_element_type=F32)
    a_buf[...] = total.astype(BF16)

    def product(i):
        loads[i].wait()
        return jnp.dot(a_buf[...], op_buf[i], preferred_element_type=F32)

    sent = []

    def combine(e, q):
        sib_copies[(e, q)].wait_recv()
        mine[e, q] += sib_in[e, q]
        if e > 0:
            value = mine[e, q]
            top = jnp.maximum(jnp.max(jnp.abs(value), axis=0, keepdims=True), 1e-30)
            far_out[e - 1, q] = jnp.round(value * (LEVELS / top)).astype(jnp.int32).astype(jnp.int16)
            top_out[e - 1, q] = top * (1.0 / LEVELS)
            copies = []
            for source, target, send, recv in (
                (far_out, far_in, far_send, far_recv), (top_out, top_in, top_send, top_recv)):
                copy = pltpu.make_async_remote_copy(
                    source.at[e - 1, q], target.at[e - 1, q], send.at[e - 1, q], recv.at[e - 1, q],
                    device_id={"wide": ahead(e, 0)}, device_id_type=MESH)
                copy.start()
                copies.append(copy)
            sent.append((e, q, copies))

    sib_copies = {}
    for n, (e, q) in enumerate(steps):
        sib_out[e, q] = product(2 * n)
        copy = pltpu.make_async_remote_copy(
            sib_out.at[e, q], sib_in.at[e, q], sib_send.at[e, q], sib_recv.at[e, q],
            device_id={"wide": ahead(0, 1)}, device_id_type=MESH)
        copy.start()
        sib_copies[(e, q)] = copy
        mine[e, q] = product(2 * n + 1)
        if n > 0:
            combine(*steps[n - 1])
    combine(*steps[-1])

    for copy in own_copies:
        copy.wait_recv()
    for e, other in pairs:
        index(e, other)
    for other in (0, 1):
        place = jnp.sum(place_buf[other], axis=1, keepdims=True) - 1.0
        for q in range(chunks // 2):
            ids = lax.broadcasted_iota(jnp.int32, (all_slots, chunk), 1) + (w * width + q * chunk)
            lands[other, :, q * chunk : (q + 1) * chunk] = (ids.astype(F32) == place).astype(F32).astype(BF16)

    nt = (((1,), (1,)), ((), ()))
    picked = jnp.zeros((2 * sensors, all_slots), F32)
    for e in range(chips):
        for q in range(chunks // 2, chunks):
            start = (q - chunks // 2) * chunk
            picked += lax.dot_general(
                split(mine[e, q]), hot[lax.rem(g + e, chips), :, start : start + chunk], nt,
                preferred_element_type=F32)
    dup_out[...] = picked[:sensors] + picked[sensors:]
    dup_copies = []
    for e, other in pairs:
        at = 2 * e + other
        copy = pltpu.make_async_remote_copy(
            dup_out, dup_in.at[at], dup_send.at[at], dup_recv.at[at],
            device_id={"wide": ahead(e, other)}, device_id_type=MESH)
        copy.start()
        dup_copies.append(copy)
    repeated = marks(own_ref[half_rows:, :], w)
    kept = 1.0 - repeated.astype(F32)
    for copy in dup_copies:
        copy.wait_recv()
    sums = [dup_out[...], None]
    for e, other in pairs:
        value = dup_in[2 * e + other]
        sums[other] = value if sums[other] is None else sums[other] + value
    sums = [split(value) for value in sums]
    for q in range(chunks // 2):
        for other in (0, 1):
            added = jnp.dot(sums[other], lands[other, :, q * chunk : (q + 1) * chunk], preferred_element_type=F32)
            mine[0, q] += added[:sensors] + added[sensors:]

    for q in range(chunks):
        value = mine[0, q]
        for e, at, copy in sent:
            if at == q:
                for part in copy:
                    part.wait_recv()
                value = value + far_in[e - 1, q].astype(jnp.int32).astype(F32) * top_in[e - 1, q]
        if q >= chunks // 2:
            first = (q - chunks // 2) * chunk // LANES
            parts = []
            for r in range(chunk // LANES):
                keep = jnp.broadcast_to(kept[first + r : first + r + 1, :], (sensors, LANES))
                parts.append(jnp.where(keep > 0.5, value[:, r * LANES : (r + 1) * LANES], 0.0))
            value = jnp.concatenate(parts, axis=1)
        out_ref[:, q * chunk : (q + 1) * chunk] = value

    for copy in adj_copies + own_copies + dup_copies + list(sib_copies.values()) + [part for s in sent for part in s[2]]:
        copy.wait_send()


def local(adjoint, operator, owner):
    wide_count, col_count = lax.axis_size("wide"), lax.axis_size("col")
    chips = wide_count // 2
    sensors, depth = adjoint.shape
    rows, block_cols = operator.shape
    width = block_cols // wide_count
    half = width // 2
    chunks = 4 if half % (2 * LANES) == 0 else 2
    chunk = width // chunks
    padded = -(-depth // LANES) * LANES
    all_slots = chips * wide_count * CAP
    pieces = (chips, chunks, sensors, chunk)
    dma = pltpu.SemaphoreType.DMA
    vmem = pl.BlockSpec(memory_space=pltpu.VMEM)
    return pl.pallas_call(
        functools.partial(kernel, wide_count, col_count, chunks),
        out_shape=jax.ShapeDtypeStruct((sensors, width), F32),
        in_specs=[vmem, pl.BlockSpec(memory_space=pl.ANY), vmem],
        out_specs=vmem,
        scratch_shapes=[
            pltpu.VMEM((wide_count * chunks, rows, chunk), BF16),
            pltpu.VMEM((col_count, sensors, padded), BF16),
            pltpu.VMEM((sensors, rows), BF16),
            pltpu.VMEM((wide_count, width // LANES, LANES), jnp.int32),
            pltpu.VMEM(pieces, F32),
            pltpu.VMEM(pieces, F32),
            pltpu.VMEM(pieces, F32),
            pltpu.VMEM((chips - 1,) + pieces[1:], jnp.int16),
            pltpu.VMEM((chips - 1,) + pieces[1:], jnp.int16),
            pltpu.VMEM((chips - 1, chunks, 1, chunk), F32),
            pltpu.VMEM((chips - 1, chunks, 1, chunk), F32),
            pltpu.VMEM((chips, all_slots, half), BF16),
            pltpu.VMEM((2, all_slots, half), BF16),
            pltpu.VMEM((2, all_slots, LANES), F32),
            pltpu.VMEM((sensors, all_slots), F32),
            pltpu.VMEM((wide_count, sensors, all_slots), F32),
            dma((wide_count * chunks,)),
            dma((col_count - 1,)), dma((col_count - 1,)),
            dma((wide_count,)), dma((wide_count,)),
            dma(pieces[:2]), dma(pieces[:2]),
            dma((chips - 1, chunks)), dma((chips - 1, chunks)),
            dma((chips - 1, chunks)), dma((chips - 1, chunks)),
            dma((wide_count,)), dma((wide_count,)),
        ],
        compiler_params=pltpu.CompilerParams(
            collective_id=0, has_side_effects=True, vmem_limit_bytes=56 * 1024 * 1024),
        cost_estimate=pl.CostEstimate(
            flops=2 * sensors * rows * block_cols, bytes_accessed=2 * rows * block_cols, transcendentals=0),
    )(adjoint, operator, owner.reshape(width // LANES, LANES))


def solution(mesh):
    return jax.shard_map(
        local,
        mesh=mesh,
        in_specs=(P(None, ("wide", "col")), P("wide", "col"), P(("col", "wide"))),
        out_specs=P(None, ("col", "wide")),
        check_vma=False,
    )
```

```python
import functools

import jax
import jax.numpy as jnp
from jax import lax
from jax.experimental import pallas as pl
from jax.experimental.pallas import tpu as pltpu
from jax.sharding import PartitionSpec as P

CAP = 16
LANES = 128
LEVELS = 32767.0
MESH = pl.DeviceIdType.MESH
F32 = jnp.float32
BF16 = jnp.bfloat16


def split(x):
    high = x.astype(BF16)
    low = (x - high.astype(F32)).astype(BF16)
    return jnp.concatenate([high, low], axis=0)


def kernel(
    wide_count, col_count, chunks,
    adj_ref, op_ref, own_ref, out_ref,
    op_buf, adj_buf, a_buf, owners, sib_out, sib_in, mine, far_out, far_in, top_out, top_in, hot, lands, place_buf, dup_out, dup_in,
    op_sem, adj_send, adj_recv, own_send, own_recv, sib_send, sib_recv, far_send, far_recv, top_send, top_recv, dup_send, dup_recv,
):
    chips = wide_count // 2
    sensors, depth = adj_ref.shape
    rows, width, chunk = op_buf.shape[1], out_ref.shape[1], op_buf.shape[2]
    half = width // 2
    half_rows = half // LANES
    slots = wide_count * CAP
    all_slots = chips * slots
    w, k = lax.axis_index("wide"), lax.axis_index("col")
    g, c = w // 2, lax.rem(w, 2)

    def ahead(e, other):
        return lax.rem(g + e, chips) * 2 + (1 - c if other else c)

    steps = [(e, q) for e in range(1, chips) for q in range(chunks)]
    steps += [(0, (q + chunks // 2) % chunks) for q in range(chunks)]
    loads = []
    for n, (e, q) in enumerate(steps):
        for other in (1, 0):
            start = pl.multiple_of(ahead(e, other) * width + q * chunk, LANES)
            i = 2 * n + 1 - other
            load = pltpu.make_async_copy(op_ref.at[:, pl.ds(start, chunk)], op_buf.at[i], op_sem.at[i])
            load.start()
            loads.append(load)

    adj_buf[k] = jnp.zeros(adj_buf.shape[1:], BF16)
    adj_buf[k, :, :depth] = adj_ref[...]
    pairs = [(e, other) for e in range(chips) for other in (0, 1)][1:]

    barrier = pltpu.get_barrier_semaphore()
    for d in range(1, col_count):
        pl.semaphore_signal(barrier, inc=1, device_id={"col": lax.rem(k + d, col_count)}, device_id_type=MESH)
    for e, other in pairs:
        pl.semaphore_signal(barrier, inc=1, device_id={"wide": ahead(e, other)}, device_id_type=MESH)
    pl.semaphore_wait(barrier, col_count - 1 + wide_count - 1)

    adj_copies = []
    for d in range(1, col_count):
        copy = pltpu.make_async_remote_copy(
            adj_buf.at[k], adj_buf.at[k], adj_send.at[d - 1], adj_recv.at[d - 1],
            device_id={"col": lax.rem(k + d, col_count)}, device_id_type=MESH)
        copy.start()
        adj_copies.append(copy)
    own_copies = []
    for e, other in pairs:
        at = 2 * e + other
        copy = pltpu.make_async_remote_copy(
            own_ref, owners.at[at], own_send.at[at], own_recv.at[at],
            device_id={"wide": ahead(e, other)}, device_id_type=MESH)
        copy.start()
        own_copies.append(copy)

    lane_in = lax.broadcasted_iota(jnp.int32, (LANES, LANES), 0)
    lane_out = lax.broadcasted_iota(jnp.int32, (LANES, LANES), 1)
    before = (lane_in < lane_out).astype(F32).astype(BF16)
    ones = jnp.ones((LANES, LANES), BF16)
    slot_ids = lax.broadcasted_iota(jnp.int32, (all_slots, LANES), 0).astype(F32)
    columns = (lax.broadcasted_iota(jnp.int32, (half_rows, LANES), 0) * LANES
               + lax.broadcasted_iota(jnp.int32, (half_rows, LANES), 1))

    def marks(owner, block):
        return owner != k * (width * wide_count) + block * width + half + columns

    def index(e, other):
        place = place_buf[other] if e > 0 else jnp.zeros((all_slots, LANES), F32)
        chip = lax.rem(g - e + chips, chips)
        block = chip * 2 + (1 - c if other else c)
        owner = own_ref[half_rows:, :] if (e, other) == (0, 0) else owners[2 * e + other, half_rows:, :]
        repeated = marks(owner, block)
        flags = repeated.astype(F32).astype(BF16)
        ranks = jnp.dot(flags, before, preferred_element_type=F32)
        counts = jnp.dot(flags, ones, preferred_element_type=F32)
        target = (owner - k * (width * wide_count) + 1).astype(F32)
        base = jnp.zeros((1, LANES), F32) + (chip * slots).astype(F32)
        for r in range(half_rows):
            slot = jnp.where(repeated[r : r + 1, :], ranks[r : r + 1, :] + base, -1.0)
            base = base + counts[r : r + 1, :]
            chosen = slot_ids == slot
            place = place + jnp.where(chosen, target[r : r + 1, :], 0.0)
            if other == 0:
                hot[chip, :, r * LANES : (r + 1) * LANES] = chosen.astype(F32).astype(BF16)
        place_buf[other] = place

    index(0, 0)

    for d in range(1, col_count):
        source = lax.rem(k - d + col_count, col_count)
        pltpu.make_async_remote_copy(
            adj_buf.at[source], adj_buf.at[source], adj_send.at[d - 1], adj_recv.at[d - 1],
            device_id={"col": source}, device_id_type=MESH).wait_recv()
    padded = adj_buf.shape[2]
    total = jnp.zeros((sensors, rows), F32)
    from_row = lax.broadcasted_iota(jnp.int32, (padded, rows), 0)
    to_row = lax.broadcasted_iota(jnp.int32, (padded, rows), 1)
    for i in range(col_count):
        shift = (from_row < depth) & (to_row == from_row + i * depth)
        total += jnp.dot(adj_buf[i], shift.astype(F32).astype(BF16), preferred_element_type=F32)
    a_buf[...] = total.astype(BF16)

    def product(i):
        loads[i].wait()
        return jnp.dot(a_buf[...], op_buf[i], preferred_element_type=F32)

    sent = []

    def combine(e, q):
        sib_copies[(e, q)].wait_recv()
        mine[e, q] += sib_in[e, q]
        if e > 0:
            value = mine[e, q]
            top = jnp.maximum(jnp.max(jnp.abs(value), axis=0, keepdims=True), 1e-30)
            far_out[e - 1, q] = jnp.round(value * (LEVELS / top)).astype(jnp.int32).astype(jnp.int16)
            top_out[e - 1, q] = top * (1.0 / LEVELS)
            copies = []
            for source, target, send, recv in (
                (far_out, far_in, far_send, far_recv), (top_out, top_in, top_send, top_recv)):
                copy = pltpu.make_async_remote_copy(
                    source.at[e - 1, q], target.at[e - 1, q], send.at[e - 1, q], recv.at[e - 1, q],
                    device_id={"wide": ahead(e, 0)}, device_id_type=MESH)
                copy.start()
                copies.append(copy)
            sent.append((e, q, copies))

    def exchange():
        for copy in own_copies:
            copy.wait_recv()
        for e, other in pairs:
            index(e, other)
        nt = (((1,), (1,)), ((), ()))
        picked = jnp.zeros((2 * sensors, all_slots), F32)
        for e in range(chips):
            for q in range(chunks // 2, chunks):
                start = (q - chunks // 2) * chunk
                picked += lax.dot_general(
                    split(mine[e, q]), hot[lax.rem(g + e, chips), :, start : start + chunk], nt,
                    preferred_element_type=F32)
        dup_out[...] = picked[:sensors] + picked[sensors:]
        dup_copies = []
        for e, other in pairs:
            at = 2 * e + other
            copy = pltpu.make_async_remote_copy(
                dup_out, dup_in.at[at], dup_send.at[at], dup_recv.at[at],
                device_id={"wide": ahead(e, other)}, device_id_type=MESH)
            copy.start()
            dup_copies.append(copy)
        return dup_copies

    sib_copies = {}
    for n, (e, q) in enumerate(steps):
        sib_out[e, q] = product(2 * n)
        copy = pltpu.make_async_remote_copy(
            sib_out.at[e, q], sib_in.at[e, q], sib_send.at[e, q], sib_recv.at[e, q],
            device_id={"wide": ahead(0, 1)}, device_id_type=MESH)
        copy.start()
        sib_copies[(e, q)] = copy
        mine[e, q] = product(2 * n + 1)
        if n > 0:
            combine(*steps[n - 1])
        if (e, q) == (0, 0):
            dup_copies = exchange()
    combine(*steps[-1])

    for other in (0, 1):
        place = jnp.sum(place_buf[other], axis=1, keepdims=True) - 1.0
        for q in range(chunks // 2):
            ids = lax.broadcasted_iota(jnp.int32, (all_slots, chunk), 1) + (w * width + q * chunk)
            lands[other, :, q * chunk : (q + 1) * chunk] = (ids.astype(F32) == place).astype(F32).astype(BF16)

    repeated = marks(own_ref[half_rows:, :], w)
    kept = 1.0 - repeated.astype(F32)
    for copy in dup_copies:
        copy.wait_recv()
    sums = [dup_out[...], None]
    for e, other in pairs:
        value = dup_in[2 * e + other]
        sums[other] = value if sums[other] is None else sums[other] + value
    sums = [split(value) for value in sums]
    for q in range(chunks // 2):
        for other in (0, 1):
            added = jnp.dot(sums[other], lands[other, :, q * chunk : (q + 1) * chunk], preferred_element_type=F32)
            mine[0, q] += added[:sensors] + added[sensors:]

    for q in range(chunks):
        value = mine[0, q]
        for e, at, copy in sent:
            if at == q:
                for part in copy:
                    part.wait_recv()
                value = value + far_in[e - 1, q].astype(jnp.int32).astype(F32) * top_in[e - 1, q]
        if q >= chunks // 2:
            first = (q - chunks // 2) * chunk // LANES
            parts = []
            for r in range(chunk // LANES):
                keep = jnp.broadcast_to(kept[first + r : first + r + 1, :], (sensors, LANES))
                parts.append(jnp.where(keep > 0.5, value[:, r * LANES : (r + 1) * LANES], 0.0))
            value = jnp.concatenate(parts, axis=1)
        out_ref[:, q * chunk : (q + 1) * chunk] = value

    for copy in adj_copies + own_copies + dup_copies + list(sib_copies.values()) + [part for s in sent for part in s[2]]:
        copy.wait_send()


def local(adjoint, operator, owner):
    wide_count, col_count = lax.axis_size("wide"), lax.axis_size("col")
    chips = wide_count // 2
    sensors, depth = adjoint.shape
    rows, block_cols = operator.shape
    width = block_cols // wide_count
    half = width // 2
    chunks = 4 if half % (2 * LANES) == 0 else 2
    chunk = width // chunks
    padded = -(-depth // LANES) * LANES
    all_slots = chips * wide_count * CAP
    pieces = (chips, chunks, sensors, chunk)
    dma = pltpu.SemaphoreType.DMA
    vmem = pl.BlockSpec(memory_space=pltpu.VMEM)
    return pl.pallas_call(
        functools.partial(kernel, wide_count, col_count, chunks),
        out_shape=jax.ShapeDtypeStruct((sensors, width), F32),
        in_specs=[vmem, pl.BlockSpec(memory_space=pl.ANY), vmem],
        out_specs=vmem,
        scratch_shapes=[
            pltpu.VMEM((wide_count * chunks, rows, chunk), BF16),
            pltpu.VMEM((col_count, sensors, padded), BF16),
            pltpu.VMEM((sensors, rows), BF16),
            pltpu.VMEM((wide_count, width // LANES, LANES), jnp.int32),
            pltpu.VMEM(pieces, F32),
            pltpu.VMEM(pieces, F32),
            pltpu.VMEM(pieces, F32),
            pltpu.VMEM((chips - 1,) + pieces[1:], jnp.int16),
            pltpu.VMEM((chips - 1,) + pieces[1:], jnp.int16),
            pltpu.VMEM((chips - 1, chunks, 1, chunk), F32),
            pltpu.VMEM((chips - 1, chunks, 1, chunk), F32),
            pltpu.VMEM((chips, all_slots, half), BF16),
            pltpu.VMEM((2, all_slots, half), BF16),
            pltpu.VMEM((2, all_slots, LANES), F32),
            pltpu.VMEM((sensors, all_slots), F32),
            pltpu.VMEM((wide_count, sensors, all_slots), F32),
            dma((wide_count * chunks,)),
            dma((col_count - 1,)), dma((col_count - 1,)),
            dma((wide_count,)), dma((wide_count,)),
            dma(pieces[:2]), dma(pieces[:2]),
            dma((chips - 1, chunks)), dma((chips - 1, chunks)),
            dma((chips - 1, chunks)), dma((chips - 1, chunks)),
            dma((wide_count,)), dma((wide_count,)),
        ],
        compiler_params=pltpu.CompilerParams(
            collective_id=0, has_side_effects=True, vmem_limit_bytes=56 * 1024 * 1024),
        cost_estimate=pl.CostEstimate(
            flops=2 * sensors * rows * block_cols, bytes_accessed=2 * rows * block_cols, transcendentals=0),
    )(adjoint, operator, owner.reshape(width // LANES, LANES))


def solution(mesh):
    return jax.shard_map(
        local,
        mesh=mesh,
        in_specs=(P(None, ("wide", "col")), P("wide", "col"), P(("col", "wide"))),
        out_specs=P(None, ("col", "wide")),
        check_vma=False,
    )
```
